256 devices in a mesh: tm: 64 (over y, x_lo, z), space: 4 (over x_hi, core).
Axes of the slice: x: 4 (x_hi: 2, x_lo: 2; x = x_hi * 2 + x_lo), y: 4, z: 8, core: 2. Of those that a mesh axis runs over, the one named last changes fastest.
Arguments:
- query: bfloat16 [512, 128, 1536], P('tm', 'space'), may hold values from -3 to 3
- key: bfloat16 [512, 128, 1536], P('tm', 'space'), may hold values from -3 to 3
- value: bfloat16 [512, 128, 1536], P('tm', 'space'), may hold values from -4 to 4
- grad_out: bfloat16 [512, 128, 1536], P('tm', 'space'), may hold values from -4 to 4
- group_order: int32 [128], replicated, may hold values from 0 to 127, as said below
- lookback: int32 [128], replicated, may hold values from 0 to 2, as said below
Outputs:
- grad_query: bfloat16 [512, 128, 1536], P('tm', 'space')
- grad_key: bfloat16 [512, 128, 1536], P('tm', 'space')
- grad_value: bfloat16 [512, 128, 1536], P('tm', 'space')
The draws below stay inside these ranges and needn't reach their ends.
Inputs may be any that keep to these rules, and one draw needn't show every extreme that they name: `group_order`: slots 2i and 2i + 1 hold groups i and 127 - i, in either order, for every i below 64. `lookback`: some group of time index 2 or more has exactly 2.
All inputs are finite; a program needn't handle non-finite values.
Results may differ from the reference program's by a relative error of at most 0.005.
Values may be sent and summed in bfloat16 or wider, within the bound.
No kernel may reach another device: no remote copies, remote signals or barrier semaphores. Data moves between devices by JAX's collectives and lax.ppermute only.
A program may use at most 128 MiB of HBM per device.

```python
import jax
import jax.numpy as jnp
from jax import lax

D = 1536
HEADS = 24
HD = 64
CH = 4
LOOK = 2
NCHUNK = 128
FRAMES = 512
PATCHES = 128


def draw_group_order(key, part):
    key = jax.random.fold_in(key, 11)
    half_count = NCHUNK // 2
    low_group = jnp.arange(half_count, dtype=jnp.int32)
    high_group = NCHUNK - 1 - low_group
    swapped = jax.random.randint(key, (half_count,), 0, 2, dtype=jnp.int32)
    first_slot = jnp.where(swapped == 1, high_group, low_group)
    second_slot = jnp.where(swapped == 1, low_group, high_group)
    return jnp.stack([first_slot, second_slot], axis=1).reshape(NCHUNK).astype(jnp.int32)


def draw_lookback(key, part):
    key = jax.random.fold_in(key, 23)
    key_values, key_place = jax.random.split(key)
    values = jax.random.randint(key_values, (NCHUNK,), 0, LOOK + 1, dtype=jnp.int32)
    where_most = jax.random.randint(key_place, (), LOOK, NCHUNK, dtype=jnp.int32)
    return values.at[where_most].set(LOOK).astype(jnp.int32)


def level_of(rng, extent, cuts, least, top_value):
    def one(position, parts):
        draws = jax.random.uniform(jax.random.fold_in(jax.random.fold_in(rng, 6), position), (parts,), jnp.float32, least / len(cuts), top_value / len(cuts))
        return jnp.repeat(jnp.exp(draws), extent[position] // parts).reshape((-1,) + (1,) * (len(extent) - position - 1))

    gain = one(*cuts[0])
    for cut in cuts[1:]:
        gain = gain * one(*cut)
    return gain


def gaussian(key, shape, scale, limit, cuts=(), kind=jnp.bfloat16):
    result = scale * jax.random.normal(key, shape, jnp.float32)
    if cuts:
        result = result * level_of(key, shape, cuts, -0.22, 0.18)
    return jnp.clip(result, -limit, limit).astype(kind)


def setup_inputs(seed: int = 0) -> dict:
    keys = jax.random.split(jax.random.key(seed), 7)
    query = gaussian(keys[0], (FRAMES, PATCHES, D), 1.0, 3.0, ((0, 64), (1, 4)))
    key = gaussian(keys[1], (FRAMES, PATCHES, D), 1.0, 3.0, ((0, 64), (1, 4)))
    value = gaussian(keys[2], (FRAMES, PATCHES, D), 1.0, 4.0, ((0, 64), (1, 4)))
    grad_out = gaussian(keys[3], (FRAMES, PATCHES, D), 1.0, 4.0, ((0, 64), (1, 4)))
    group_order = draw_group_order(jax.random.fold_in(keys[6], 71), 0)
    lookback = draw_lookback(jax.random.fold_in(keys[6], 71), 0)
    return {"query": query, "key": key, "value": value, "grad_out": grad_out, "group_order": group_order, "lookback": lookback}


def attend_grads(query_rows, key_rows, value_rows, grad_rows, allowed, factor):
    query_full = query_rows.astype(jnp.float32)
    key_full = key_rows.astype(jnp.float32)
    value_full = value_rows.astype(jnp.float32)
    grad_full = grad_rows.astype(jnp.float32)
    scores = jnp.einsum("bqhe,bkhe->bhqk", query_full, key_full) * factor
    unnormed = jnp.where(allowed[:, None], jnp.exp(scores), 0.0)
    totals = jnp.sum(unnormed, axis=-1)
    grad_probs = jnp.einsum("bqhe,bkhe->bhqk", grad_full, value_full)
    row_delta = jnp.sum(unnormed * grad_probs, axis=-1) / totals
    prob_full = unnormed / totals[..., None]
    prob_half = lax.optimization_barrier(prob_full.astype(jnp.bfloat16)).astype(jnp.float32)
    grad_scores = lax.optimization_barrier(
        (prob_full * (grad_probs - row_delta[..., None]) * factor).astype(jnp.bfloat16)).astype(jnp.float32)
    grad_query = jnp.einsum("bhqk,bkhe->bqhe", grad_scores, key_full)
    grad_key = jnp.einsum("bhqk,bqhe->bkhe", grad_scores, query_full)
    grad_value = jnp.einsum("bhqk,bqhe->bkhe", prob_half, grad_full)
    return grad_query, grad_key, grad_value


def reference(query, key, value, grad_out, group_order, lookback):
    factor = HD ** -0.5
    half_width = D // 2
    head_count = HEADS // 2
    frames = query.shape[0]
    patches = query.shape[1]
    group_count = group_order.shape[0]
    frame_block = 2 * CH
    block_count = frames // frame_block

    def spatial_view(source):
        return source[:, :, :half_width].reshape(block_count, frame_block, patches, head_count, HD)

    everywhere = jnp.zeros((1, patches, patches), jnp.int32) == 0

    def spatial_block(pieces):
        return attend_grads(pieces[0], pieces[1], pieces[2], pieces[3], everywhere, factor)

    spatial_dq, spatial_dk, spatial_dv = lax.map(
        spatial_block, (spatial_view(query), spatial_view(key), spatial_view(value), spatial_view(grad_out)))

    slot_of = jnp.zeros((group_count,), jnp.int32).at[group_order].set(jnp.arange(group_count, dtype=jnp.int32))

    def time_view(source):
        return source[:, :, half_width:].reshape(group_count, CH, patches, head_count, HD)[slot_of]

    time_query = time_view(query)
    time_key = time_view(key)
    time_value = time_view(value)
    time_grad = time_view(grad_out)
    padding = jnp.zeros((LOOK,) + time_key.shape[1:], time_key.dtype)
    key_padded = jnp.concatenate([padding, time_key], axis=0)
    value_padded = jnp.concatenate([padding, time_value], axis=0)
    window_rows = (LOOK + 1) * CH
    key_offsets = jnp.arange(LOOK + 1, dtype=jnp.int32)

    def one_group(state_pair, group):
        key_sums, value_sums = state_pair
        key_window = lax.dynamic_slice_in_dim(key_padded, group, LOOK + 1, 0).reshape(
            window_rows, patches, head_count, HD)
        value_window = lax.dynamic_slice_in_dim(value_padded, group, LOOK + 1, 0).reshape(
            window_rows, patches, head_count, HD)
        query_now = lax.dynamic_index_in_dim(time_query, group, 0, keepdims=False)
        grad_now = lax.dynamic_index_in_dim(time_grad, group, 0, keepdims=False)
        key_groups = group - LOOK + key_offsets
        usable = (key_groups >= 0) & (key_groups >= group - lookback[group])
        allowed = jnp.broadcast_to(
            jnp.repeat(usable, CH, total_repeat_length=window_rows)[None, None, :], (1, CH, window_rows))
        grad_query, grad_key, grad_value = attend_grads(
            jnp.swapaxes(query_now, 0, 1), jnp.swapaxes(key_window, 0, 1),
            jnp.swapaxes(value_window, 0, 1), jnp.swapaxes(grad_now, 0, 1), allowed, factor)
        key_part = jnp.swapaxes(grad_key, 0, 1).reshape(LOOK + 1, CH, patches, head_count, HD)
        value_part = jnp.swapaxes(grad_value, 0, 1).reshape(LOOK + 1, CH, patches, head_count, HD)
        current_key = lax.dynamic_slice_in_dim(key_sums, group, LOOK + 1, 0)
        current_value = lax.dynamic_slice_in_dim(value_sums, group, LOOK + 1, 0)
        key_sums = lax.dynamic_update_slice_in_dim(key_sums, current_key + key_part, group, 0)
        value_sums = lax.dynamic_update_slice_in_dim(value_sums, current_value + value_part, group, 0)
        return (key_sums, value_sums), jnp.swapaxes(grad_query, 0, 1)

    empty_sums = jnp.zeros((group_count + LOOK, CH, patches, head_count, HD), jnp.float32)
    (key_sums, value_sums), time_dq = lax.scan(
        one_group, (empty_sums, empty_sums), jnp.arange(group_count, dtype=jnp.int32))

    def slot_view(time_array):
        return time_array[group_order].reshape(frames, patches, half_width)

    grad_query = jnp.concatenate(
        [spatial_dq.reshape(frames, patches, half_width), slot_view(time_dq)], axis=2).astype(jnp.bfloat16)
    grad_key = jnp.concatenate(
        [spatial_dk.reshape(frames, patches, half_width), slot_view(key_sums[LOOK:])], axis=2).astype(jnp.bfloat16)
    grad_value = jnp.concatenate(
        [spatial_dv.reshape(frames, patches, half_width), slot_view(value_sums[LOOK:])], axis=2).astype(jnp.bfloat16)
    return (grad_query, grad_key, grad_value)
```

```python
import functools

import jax
import jax.numpy as jnp
from jax import lax
from jax.experimental import pallas as pl
from jax.experimental.pallas import tpu as pltpu
from jax.sharding import PartitionSpec as P

HD = 64
LANES = 2 * HD
FACTOR = HD**-0.5
VMEM_LIMIT = 48 * 1024 * 1024
BF16 = jnp.bfloat16
F32 = jnp.float32


def params(**kwargs):
    return pltpu.CompilerParams(vmem_limit_bytes=VMEM_LIMIT, **kwargs)


def chain_swap(value, phase):
    count = lax.axis_size("tm")
    pairs = []
    for source in range(count):
        target = source ^ 1 if phase == 0 else ((source + 1) ^ 1) - 1
        if target == count:
            target = source
        if target >= 0:
            pairs.append((source, target))
    return lax.ppermute(value, "tm", pairs)


def space_swap(value, flip):
    count = lax.axis_size("space")
    return lax.ppermute(value, "space", [(i, i ^ flip) for i in range(count)])


def side_slots(order_ref):
    device = lax.axis_index("tm")
    early_slot = jnp.where(order_ref[2 * device] == device, 0, 1)
    odd = lax.rem(device, 2)
    slot0 = jnp.where(odd == 1, early_slot, 1 - early_slot)
    return slot0, 1 - slot0


def side_groups(entries):
    device = lax.axis_index("tm")
    odd = lax.rem(device, 2)
    late = entries - 1 - device
    return jnp.where(odd == 1, device, late), jnp.where(odd == 1, late, device)


def pack_chain_kernel(order_ref, key_ref, value_ref, out0_ref, out1_ref, sems):
    slot0, slot1 = side_slots(order_ref)
    frames, _, width = key_ref.shape
    half, cols = frames // 2, pl.ds(width // 2, width // 2)
    copies = []
    for index, (slot, out_ref) in enumerate(((slot1, out0_ref), (slot0, out1_ref))):
        for part, source in enumerate((key_ref, value_ref)):
            copies.append(
                pltpu.make_async_copy(
                    source.at[pl.ds(slot * half, half), :, cols],
                    out_ref.at[part],
                    sems.at[2 * index + part],
                )
            )
    for copy in copies:
        copy.start()
    for copy in copies:
        copy.wait()


def pack_chain(group_order, key, value):
    frames, patches, width = key.shape
    shape = jax.ShapeDtypeStruct((2, frames // 2, patches, width // 2), BF16)
    return pl.pallas_call(
        pack_chain_kernel,
        out_shape=(shape, shape),
        in_specs=[pl.BlockSpec(memory_space=pltpu.SMEM)] + [pl.BlockSpec(memory_space=pl.ANY)] * 2,
        out_specs=[pl.BlockSpec(memory_space=pl.ANY)] * 2,
        scratch_shapes=[pltpu.SemaphoreType.DMA((4,))],
        compiler_params=params(),
        name="pack_chain",
    )(group_order, key, value)


def pack_space_kernel(*refs):
    arrays, outs, sems = refs[:4], refs[4:7], refs[7]
    me = lax.axis_index("space")
    _, _, width = arrays[0].shape
    share = outs[0].shape[1]
    copies = []
    for index, out_ref in enumerate(outs):
        other = me ^ (index + 1)
        for part, source in enumerate(arrays):
            copies.append(
                pltpu.make_async_copy(
                    source.at[pl.ds(other * share, share), :, pl.ds(0, width // 2)],
                    out_ref.at[part],
                    sems.at[4 * index + part],
                )
            )
    for copy in copies:
        copy.start()
    for copy in copies:
        copy.wait()


def pack_space(query, key, value, grad):
    frames, patches, width = key.shape
    shape = jax.ShapeDtypeStruct((4, frames // 4, patches, width // 2), BF16)
    return pl.pallas_call(
        pack_space_kernel,
        out_shape=(shape,) * 3,
        in_specs=[pl.BlockSpec(memory_space=pl.ANY)] * 4,
        out_specs=[pl.BlockSpec(memory_space=pl.ANY)] * 3,
        scratch_shapes=[pltpu.SemaphoreType.DMA((12,))],
        compiler_params=params(),
        name="pack_space",
    )(query, key, value, grad)


def two_heads(rows):
    first = lax.broadcasted_iota(jnp.int32, rows.shape, 1) < HD
    zero = jnp.zeros_like(rows)
    return jnp.concatenate([jnp.where(first, rows, zero), jnp.where(first, zero, rows)], axis=0)


def rows_by_rows(left, right):
    return lax.dot_general(left, right, (((1,), (1,)), ((), ())), preferred_element_type=F32)


def attend(query, grad, blocks):
    scaled2 = two_heads(query * jnp.asarray(FACTOR, BF16))
    grad2 = two_heads(grad)
    unnormed, probs = [], []
    totals = weighted = None
    for key, value, weight in blocks:
        part = jnp.exp(rows_by_rows(key, scaled2))
        if weight is not None:
            part = part * weight
        grad_probs = rows_by_rows(value, grad2)
        total = jnp.sum(part, axis=0, keepdims=True)
        weigh = jnp.sum(part * grad_probs, axis=0, keepdims=True)
        totals = total if totals is None else totals + total
        weighted = weigh if weighted is None else weighted + weigh
        unnormed.append(part)
        probs.append(grad_probs)
    inverse = 1.0 / totals
    delta = weighted * inverse
    grad_query, grad_blocks = None, []
    for (key, _, _), part, grad_probs in zip(blocks, unnormed, probs):
        prob = part * inverse
        grad_scores = (prob * (grad_probs - delta)).astype(BF16)
        grad_value = jnp.dot(prob.astype(BF16), grad2, preferred_element_type=F32)
        grad_key = jnp.dot(grad_scores, scaled2, preferred_element_type=F32)
        piece = lax.dot_general(
            grad_scores, key, (((0,), (0,)), ((), ())), preferred_element_type=F32
        )
        grad_query = piece if grad_query is None else grad_query + piece
        grad_blocks.append((grad_key, grad_value))
    rows = query.shape[0]
    first = lax.broadcasted_iota(jnp.int32, (rows, LANES), 1) < HD
    grad_query = jnp.where(first, grad_query[:rows], grad_query[rows:]) * FACTOR
    return grad_query, grad_blocks


def chain_kernel(
    order_ref,
    lookback_ref,
    query_ref,
    key_ref,
    value_ref,
    grad_ref,
    near0_ref,
    near1_ref,
    far0_ref,
    far1_ref,
    dq_ref,
    own_ref,
    dnear0_ref,
    dnear1_ref,
    dfar0_ref,
    dfar1_ref,
):
    frames, patches, _ = query_ref.shape
    half = frames // 2
    rows = half * patches
    flat, tall = (rows, LANES), (half, patches, LANES)
    slots = side_slots(order_ref)
    groups = side_groups(order_ref.shape[0])
    key_patch = lax.rem(lax.broadcasted_iota(jnp.int32, (rows, 2 * rows), 0), patches)
    query_patch = lax.rem(lax.broadcasted_iota(jnp.int32, (rows, 2 * rows), 1), patches)
    same = (key_patch == query_patch).astype(F32)
    sides = ((near0_ref, far0_ref, dnear0_ref, dfar0_ref), (near1_ref, far1_ref, dnear1_ref, dfar1_ref))
    for slot, group, (near_ref, far_ref, dnear_ref, dfar_ref) in zip(slots, groups, sides):
        reach = jnp.minimum(lookback_ref[group], group)
        near_weight = same * jnp.where(reach >= 1, 1.0, 0.0)
        far_weight = same * jnp.where(reach >= 2, 1.0, 0.0)
        mine = pl.ds(slot * half, half)
        grad_query, ((dk, dv), (dk_near, dv_near), (dk_far, dv_far)) = attend(
            query_ref[mine].reshape(flat),
            grad_ref[mine].reshape(flat),
            (
                (key_ref[mine].reshape(flat), value_ref[mine].reshape(flat), same),
                (near_ref[0].reshape(flat), near_ref[1].reshape(flat), near_weight),
                (far_ref[0].reshape(flat), far_ref[1].reshape(flat), far_weight),
            ),
        )
        dq_ref[mine] = grad_query.astype(BF16).reshape(tall)
        own_ref[0, mine] = dk.reshape(tall)
        own_ref[1, mine] = dv.reshape(tall)
        dnear_ref[0] = dk_near.reshape(tall)
        dnear_ref[1] = dv_near.reshape(tall)
        dfar_ref[0] = dk_far.astype(BF16).reshape(tall)
        dfar_ref[1] = dv_far.astype(BF16).reshape(tall)


def chain_grads(group_order, lookback, query, key, value, grad, near0, near1, far0, far1):
    frames, patches, width = query.shape
    half, columns = frames // 2, width // 2
    steps = columns // LANES
    whole = pl.BlockSpec((frames, patches, LANES), lambda i, *_: (0, 0, steps + i))
    pair = pl.BlockSpec((2, half, patches, LANES), lambda i, *_: (0, 0, 0, i))
    pair_shape = (2, half, patches, columns)
    return pl.pallas_call(
        chain_kernel,
        grid_spec=pltpu.PrefetchScalarGridSpec(
            num_scalar_prefetch=2,
            grid=(steps,),
            in_specs=[whole] * 4 + [pair] * 4,
            out_specs=[
                pl.BlockSpec((frames, patches, LANES), lambda i, *_: (0, 0, i)),
                pl.BlockSpec((2, frames, patches, LANES), lambda i, *_: (0, 0, 0, i)),
            ]
            + [pair] * 4,
        ),
        out_shape=[
            jax.ShapeDtypeStruct((frames, patches, columns), BF16),
            jax.ShapeDtypeStruct((2, frames, patches, columns), F32),
            jax.ShapeDtypeStruct(pair_shape, F32),
            jax.ShapeDtypeStruct(pair_shape, F32),
            jax.ShapeDtypeStruct(pair_shape, BF16),
            jax.ShapeDtypeStruct(pair_shape, BF16),
        ],
        compiler_params=params(),
        cost_estimate=pl.CostEstimate(
            flops=800_000_000, bytes_accessed=8_000_000, transcendentals=1_200_000
        ),
        name="chain_grads",
    )(group_order, lookback, query, key, value, grad, near0, near1, far0, far1)


def space_kernel(
    query_ref, key_ref, value_ref, grad_ref, in1_ref, in2_ref, in3_ref, out0_ref, out1_ref, out2_ref, out3_ref
):
    me = lax.axis_index("space")
    share, patches = in1_ref.shape[1], in1_ref.shape[2]
    outs = (out0_ref, out1_ref, out2_ref, out3_ref)
    for frame in range(share):
        gathered = [
            jnp.concatenate(
                [own_ref[share * me + frame]] + [ref[part, frame] for ref in (in1_ref, in2_ref, in3_ref)],
                axis=0,
            )
            for part, own_ref in enumerate((query_ref, key_ref, value_ref, grad_ref))
        ]
        query, key, value, grad = gathered
        grad_query, ((grad_key, grad_value),) = attend(query, grad, ((key, value, None),))
        for part, result in enumerate((grad_query, grad_key, grad_value)):
            result = result.astype(BF16)
            for place, out_ref in enumerate(outs):
                out_ref[part, frame] = result[place * patches : (place + 1) * patches]


def space_grads(query, key, value, grad, arrived):
    frames, patches, width = query.shape
    share, columns = frames // 4, width // 2
    own = pl.BlockSpec((frames, patches, LANES), lambda i: (0, 0, i))
    return pl.pallas_call(
        space_kernel,
        grid=(columns // LANES,),
        in_specs=[own] * 4 + [pl.BlockSpec((4, share, patches, LANES), lambda i: (0, 0, 0, i))] * 3,
        out_specs=[pl.BlockSpec((3, share, patches, LANES), lambda i: (0, 0, 0, i))] * 4,
        out_shape=[jax.ShapeDtypeStruct((3, share, patches, columns), BF16)] * 4,
        compiler_params=params(),
        cost_estimate=pl.CostEstimate(
            flops=400_000_000, bytes_accessed=4_000_000, transcendentals=400_000
        ),
        name="space_grads",
    )(query, key, value, grad, *arrived)


def finish_kernel(steps, order_ref, *refs):
    parts, (dq_ref, own_ref, got0_ref, got1_ref), outs = refs[:4], refs[4:8], refs[8:]
    step = pl.program_id(0)
    share, frames = parts[0].shape[1], dq_ref.shape[0]
    half = frames // 2

    @pl.when(step < steps)
    def _():
        me = lax.axis_index("space")
        for flip, part_ref in enumerate(parts):
            place = pl.ds(share * (me ^ flip), share)
            for index, out_ref in enumerate(outs):
                out_ref[place] = part_ref[index]

    @pl.when(step >= steps)
    def _():
        outs[0][...] = dq_ref[...]
        for slot, got_ref in zip(side_slots(order_ref), (got0_ref, got1_ref)):
            mine = pl.ds(slot * half, half)
            for index in range(2):
                total = own_ref[index, mine] + got_ref[index].astype(F32)
                outs[1 + index][mine] = total.astype(BF16)


def finish(group_order, parts, dq, own, got0, got1):
    frames, patches, columns = dq.shape
    wide = 3 * LANES
    steps = columns // wide
    share = parts[0].shape[1]

    def early(i, *_):
        return (0, 0, 0, jnp.minimum(i, steps - 1))

    def late(i, *_):
        return (0, 0, 0, jnp.maximum(i - steps, 0))

    return pl.pallas_call(
        functools.partial(finish_kernel, steps),
        grid_spec=pltpu.PrefetchScalarGridSpec(
            num_scalar_prefetch=1,
            grid=(2 * steps,),
            in_specs=[pl.BlockSpec((3, share, patches, wide), early)] * 4
            + [
                pl.BlockSpec((frames, patches, wide), lambda i, *_: (0, 0, jnp.maximum(i - steps, 0))),
                pl.BlockSpec((2, frames, patches, wide), late),
                pl.BlockSpec((2, frames // 2, patches, wide), late),
                pl.BlockSpec((2, frames // 2, patches, wide), late),
            ],
            out_specs=[pl.BlockSpec((frames, patches, wide), lambda i, *_: (0, 0, i))] * 3,
        ),
        out_shape=[jax.ShapeDtypeStruct((frames, patches, 2 * columns), BF16)] * 3,
        compiler_params=params(),
        name="finish",
    )(group_order, *parts, dq, own, got0, got1)


def on_device(query, key, value, grad_out, group_order, lookback):
    chain0, chain1 = pack_chain(group_order, key, value)
    near0 = chain_swap(chain0, 0)
    near1 = chain_swap(chain1, 1)
    sent = pack_space(query, key, value, grad_out)
    arrived = [space_swap(part, flip) for flip, part in enumerate(sent, 1)]
    far1 = chain_swap(near0, 1)
    far0 = chain_swap(near1, 0)
    dq, own, dnear0, dnear1, dfar0, dfar1 = chain_grads(
        group_order, lookback, query, key, value, grad_out, near0, near1, far0, far1
    )
    back1 = chain_swap(dfar0, 0)
    back0 = chain_swap(dfar1, 1)
    results = space_grads(query, key, value, grad_out, arrived)
    parts = [results[0]] + [space_swap(part, flip) for flip, part in enumerate(results[1:], 1)]
    got0 = chain_swap((dnear1 + back1.astype(F32)).astype(BF16), 1)
    got1 = chain_swap((dnear0 + back0.astype(F32)).astype(BF16), 0)
    return tuple(finish(group_order, parts, dq, own, got0, got1))


def solution(mesh):
    spread = P("tm", "space", None)
    return jax.shard_map(
        on_device,
        mesh=mesh,
        in_specs=(spread,) * 4 + (P(), P()),
        out_specs=(spread,) * 3,
        check_vma=False,
    )
```

```python
import functools

import jax
import jax.numpy as jnp
from jax import lax
from jax.experimental import pallas as pl
from jax.experimental.pallas import tpu as pltpu
from jax.sharding import PartitionSpec as P

HD = 64
LANES = 2 * HD
CHAIN_LANES = 4 * HD
SPACE_LANES = 12 * HD
BAND = 16
FACTOR = HD**-0.5
VMEM_LIMIT = 48 * 1024 * 1024
BF16 = jnp.bfloat16
F32 = jnp.float32


def params(**kwargs):
    return pltpu.CompilerParams(vmem_limit_bytes=VMEM_LIMIT, **kwargs)


def chain_swap(value, phase):
    count = lax.axis_size("tm")
    pairs = []
    for source in range(count):
        target = source ^ 1 if phase == 0 else ((source + 1) ^ 1) - 1
        if target == count:
            target = source
        if target >= 0:
            pairs.append((source, target))
    return lax.ppermute(value, "tm", pairs)


def space_swap(value, flip):
    count = lax.axis_size("space")
    return lax.ppermute(value, "space", [(i, i ^ flip) for i in range(count)])


def side_slots(order_ref):
    device = lax.axis_index("tm")
    early_slot = jnp.where(order_ref[2 * device] == device, 0, 1)
    odd = lax.rem(device, 2)
    slot0 = jnp.where(odd == 1, early_slot, 1 - early_slot)
    return slot0, 1 - slot0


def side_groups(entries):
    device = lax.axis_index("tm")
    odd = lax.rem(device, 2)
    late = entries - 1 - device
    return jnp.where(odd == 1, device, late), jnp.where(odd == 1, late, device)


def pack_kernel(order_ref, query_ref, key_ref, value_ref, grad_ref, *refs):
    chain_refs, space_refs, sems = refs[:2], refs[2:5], refs[5]
    slot0, slot1 = side_slots(order_ref)
    me = lax.axis_index("space")
    frames, _, width = key_ref.shape
    half, share, columns = frames // 2, frames // 4, width // 2
    copies = []

    def send(source, first, count, column, target):
        piece = source.at[pl.ds(first, count), :, pl.ds(column, columns)]
        copies.append(pltpu.make_async_copy(piece, target, sems.at[len(copies)]))

    for here, there, out_ref in ((slot0, slot1, chain_refs[0]), (slot1, slot0, chain_refs[1])):
        send(key_ref, there * half, half, columns, out_ref.at[0])
        send(value_ref, there * half, half, columns, out_ref.at[1])
        send(query_ref, here * half, half, columns, out_ref.at[2])
        send(grad_ref, here * half, half, columns, out_ref.at[3])
    for flip, out_ref in enumerate(space_refs, 1):
        for part, source in enumerate((query_ref, key_ref, value_ref, grad_ref)):
            send(source, (me ^ flip) * share, share, 0, out_ref.at[part])
    for copy in copies:
        copy.start()
    for copy in copies:
        copy.wait()


def pack(group_order, query, key, value, grad):
    frames, patches, width = key.shape
    chain = jax.ShapeDtypeStruct((4, frames // 2, patches, width // 2), BF16)
    space = jax.ShapeDtypeStruct((4, frames // 4, patches, width // 2), BF16)
    outs = pl.pallas_call(
        pack_kernel,
        out_shape=(chain, chain, space, space, space),
        in_specs=[pl.BlockSpec(memory_space=pltpu.SMEM)] + [pl.BlockSpec(memory_space=pl.ANY)] * 4,
        out_specs=[pl.BlockSpec(memory_space=pl.ANY)] * 5,
        scratch_shapes=[pltpu.SemaphoreType.DMA((20,))],
        compiler_params=params(),
        name="pack",
    )(group_order, *[pltpu.with_memory_space_constraint(x, pltpu.HBM) for x in (query, key, value, grad)])
    return outs[:2], outs[2:]


def per_head(rows):
    head = lax.broadcasted_iota(jnp.int32, rows.shape, 1) // HD
    zero = jnp.zeros_like(rows)
    return jnp.concatenate([jnp.where(head == h, rows, zero) for h in range(rows.shape[1] // HD)], axis=0)


def own_head(bands):
    heads = bands.shape[1] // HD
    rows = bands.shape[0] // heads
    head = lax.broadcasted_iota(jnp.int32, (rows, bands.shape[1]), 1) // HD
    result = bands[:rows]
    for h in range(1, heads):
        result = jnp.where(head == h, bands[h * rows : (h + 1) * rows], result)
    return result


BY_ROWS = (((1,), (1,)), ((), ()))
BY_COLUMNS = (((0,), (0,)), ((), ()))


def pairs(key, value, scaled, grads, weight):
    unnormed = jnp.exp(lax.dot_general(key, scaled, BY_ROWS, preferred_element_type=F32))
    if weight is not None:
        unnormed = unnormed * weight
    return unnormed, lax.dot_general(value, grads, BY_ROWS, preferred_element_type=F32)


def sums(unnormed, grad_probs):
    return jnp.sum(unnormed, axis=0, keepdims=True), jnp.sum(unnormed * grad_probs, axis=0, keepdims=True)


def gradients(key, scaled, grads, unnormed, grad_probs, totals, weighted):
    inverse = jnp.where(totals > 0.0, 1.0 / totals, 0.0)
    prob = unnormed * inverse
    grad_scores = (prob * (grad_probs - weighted * inverse)).astype(BF16)
    grad_value = jnp.dot(prob.astype(BF16), grads, preferred_element_type=F32)
    grad_key = jnp.dot(grad_scores, scaled, preferred_element_type=F32)
    bands = lax.dot_general(grad_scores, key, BY_COLUMNS, preferred_element_type=F32)
    return own_head(bands) * FACTOR, grad_key, grad_value


def scale(query):
    return per_head(query * jnp.asarray(FACTOR, BF16))


def attend(query, key, value, grad):
    scaled, grads = scale(query), per_head(grad)
    unnormed, grad_probs = pairs(key, value, scaled, grads, None)
    return gradients(key, scaled, grads, unnormed, grad_probs, *sums(unnormed, grad_probs))


class Side:
    def __init__(self, side, order_ref, lookback_ref, locals_, before_ref, after_ref):
        self.locals, self.before, self.after = locals_, before_ref, after_ref
        frames, self.patches, self.lanes = locals_[0].shape
        self.half = frames // 2
        self.rows = self.half * BAND
        self.heads = self.lanes // HD
        self.mine = pl.ds(side_slots(order_ref)[side] * self.half, self.half)
        entries = order_ref.shape[0]
        group = side_groups(entries)[side]
        reach = jnp.minimum(lookback_ref[group], group)
        following = jnp.minimum(group + 1, entries - 1)
        reach_after = jnp.where(group + 1 < entries, jnp.minimum(lookback_ref[following], following), 0)
        shape = (2 * self.rows, self.heads * self.rows)
        key_row = lax.broadcasted_iota(jnp.int32, shape, 0)
        query_row = lax.broadcasted_iota(jnp.int32, shape, 1)
        same = lax.rem(key_row, BAND) == lax.rem(query_row, BAND)
        allowed = same & (key_row // self.rows <= reach)
        self.weight = jnp.where(allowed, 1.0, 0.0)
        self.skip_weight = jnp.where(same & (reach_after >= 2), 1.0, 0.0)[: self.rows]

    def flat(self, piece):
        return piece.reshape(self.rows, self.lanes)

    def load(self, band):
        at = pl.ds(band * BAND, BAND)
        query, key, value, grad = (self.flat(ref[self.mine, at]) for ref in self.locals)
        key_before, value_before = (self.flat(self.before[index, :, at]) for index in (0, 1))
        query_after, grad_after = (self.flat(self.after[index, :, at]) for index in (2, 3))
        keys = jnp.concatenate([key, key_before], axis=0)
        values = jnp.concatenate([value, value_before], axis=0)
        near = (keys, scale(query), per_head(grad))
        skip = (key_before, scale(query_after), per_head(grad_after))
        near_pairs = pairs(keys, values, near[1], near[2], self.weight)
        skip_pairs = pairs(key_before, value_before, skip[1], skip[2], self.skip_weight)
        return near + near_pairs, skip + skip_pairs


def both_sides(order_ref, lookback_ref, locals_, got0_ref, got1_ref):
    return (
        Side(0, order_ref, lookback_ref, locals_, got0_ref, got1_ref),
        Side(1, order_ref, lookback_ref, locals_, got1_ref, got0_ref),
    )


def chain_sums_kernel(
    order_ref, lookback_ref, query_ref, key_ref, value_ref, grad_ref, got0_ref, got1_ref, out0_ref, out1_ref
):
    sides = both_sides(order_ref, lookback_ref, (query_ref, key_ref, value_ref, grad_ref), got0_ref, got1_ref)
    for side, near_out, skip_out in zip(sides, (out0_ref, out1_ref), (out1_ref, out0_ref)):
        for band in range(side.patches // BAND):
            near, skip = side.load(band)
            near_out[0, band, 0:1], near_out[0, band, 1:2] = sums(*near[3:])
            skip_out[0, band, 2:3], skip_out[0, band, 3:4] = sums(*skip[3:])


def chain_grads_kernel(
    order_ref,
    lookback_ref,
    query_ref,
    key_ref,
    value_ref,
    grad_ref,
    got0_ref,
    got1_ref,
    sums0_ref,
    sums1_ref,
    from0_ref,
    from1_ref,
    own_ref,
    out0_ref,
    out1_ref,
):
    sides = both_sides(order_ref, lookback_ref, (query_ref, key_ref, value_ref, grad_ref), got0_ref, got1_ref)
    mine, others, outs = (sums0_ref, sums1_ref), (from0_ref, from1_ref), (out0_ref, out1_ref)
    for number, side in enumerate(sides):
        rows, tall = side.rows, (side.half, BAND, side.lanes)
        for band in range(side.patches // BAND):
            at = pl.ds(band * BAND, BAND)
            near, skip = side.load(band)

            def whole_sums(row):
                place = number if row == 0 else 1 - number
                ours, theirs = mine[place], others[place]
                return [
                    ours[0, band, row + k : row + k + 1] + theirs[0, band, 2 - row + k : 3 - row + k] for k in (0, 1)
                ]

            dq, dk, dv = gradients(*near, *whole_sums(0))
            dq_after, dk_before, dv_before = gradients(*skip, *whole_sums(2))
            own_ref[0, side.mine, at] = dq.reshape(tall)
            own_ref[1, side.mine, at] = dk[:rows].reshape(tall)
            own_ref[2, side.mine, at] = dv[:rows].reshape(tall)
            back, on = outs[number], outs[1 - number]
            back[0, :, at] = (dk[rows:] + dk_before).astype(BF16).reshape(tall)
            back[1, :, at] = (dv[rows:] + dv_before).astype(BF16).reshape(tall)
            on[2, :, at] = dq_after.astype(BF16).reshape(tall)


def chain_specs(query):
    frames, patches, width = query.shape
    half, columns = frames // 2, width // 2
    steps = columns // CHAIN_LANES
    bands = patches // BAND
    wide = CHAIN_LANES // HD * half * BAND
    whole = pl.BlockSpec((frames, patches, CHAIN_LANES), lambda i, *_: (0, 0, steps + i))
    got = pl.BlockSpec((4, half, patches, CHAIN_LANES), lambda i, *_: (0, 0, 0, i))
    part = pl.BlockSpec((1, bands, 4, wide), lambda i, *_: (i, 0, 0, 0))
    return steps, [whole] * 4 + [got] * 2, part, jax.ShapeDtypeStruct((steps, bands, 4, wide), F32)


def chain_sums(group_order, lookback, query, key, value, grad, got0, got1):
    steps, in_specs, part, shape = chain_specs(query)
    return pl.pallas_call(
        chain_sums_kernel,
        grid_spec=pltpu.PrefetchScalarGridSpec(
            num_scalar_prefetch=2, grid=(steps,), in_specs=in_specs, out_specs=[part] * 2
        ),
        out_shape=[shape] * 2,
        compiler_params=params(),
        name="chain_sums",
    )(group_order, lookback, query, key, value, grad, got0, got1)


def chain_grads(group_order, lookback, query, key, value, grad, got0, got1, ours, theirs):
    frames, patches, width = query.shape
    half, columns = frames // 2, width // 2
    steps, in_specs, part, _ = chain_specs(query)
    sent = jax.ShapeDtypeStruct((3, half, patches, columns), BF16)
    return pl.pallas_call(
        chain_grads_kernel,
        grid_spec=pltpu.PrefetchScalarGridSpec(
            num_scalar_prefetch=2,
            grid=(steps,),
            in_specs=in_specs + [part] * 4,
            out_specs=[pl.BlockSpec((3, frames, patches, CHAIN_LANES), lambda i, *_: (0, 0, 0, i))]
            + [pl.BlockSpec((3, half, patches, CHAIN_LANES), lambda i, *_: (0, 0, 0, i))] * 2,
        ),
        out_shape=[jax.ShapeDtypeStruct((3, frames, patches, columns), F32), sent, sent],
        compiler_params=params(),
        name="chain_grads",
    )(group_order, lookback, query, key, value, grad, got0, got1, *ours, *theirs)


def space_kernel(
    query_ref, key_ref, value_ref, grad_ref, in1_ref, in2_ref, in3_ref, out0_ref, out1_ref, out2_ref, out3_ref
):
    me = lax.axis_index("space")
    share, patches = in1_ref.shape[1], in1_ref.shape[2]
    outs = (out0_ref, out1_ref, out2_ref, out3_ref)
    for frame in range(share):
        gathered = [
            jnp.concatenate(
                [own_ref[share * me + frame]] + [ref[part, frame] for ref in (in1_ref, in2_ref, in3_ref)],
                axis=0,
            )
            for part, own_ref in enumerate((query_ref, key_ref, value_ref, grad_ref))
        ]
        couples = [
            attend(*(rows[:, c : c + LANES] for rows in gathered))
            for c in range(0, gathered[0].shape[1], LANES)
        ]
        grad_query, grad_key, grad_value = (jnp.concatenate(x, axis=1) for x in zip(*couples))
        for part, result in enumerate((grad_query, grad_key, grad_value)):
            result = result.astype(BF16)
            for place, out_ref in enumerate(outs):
                out_ref[part, frame] = result[place * patches : (place + 1) * patches]


def space_grads(query, key, value, grad, arrived):
    frames, patches, width = query.shape
    share, columns = frames // 4, width // 2
    own = pl.BlockSpec((frames, patches, SPACE_LANES), lambda i: (0, 0, i))
    return pl.pallas_call(
        space_kernel,
        grid=(columns // SPACE_LANES,),
        in_specs=[own] * 4 + [pl.BlockSpec((4, share, patches, SPACE_LANES), lambda i: (0, 0, 0, i))] * 3,
        out_specs=[pl.BlockSpec((3, share, patches, SPACE_LANES), lambda i: (0, 0, 0, i))] * 4,
        out_shape=[jax.ShapeDtypeStruct((3, share, patches, columns), BF16)] * 4,
        compiler_params=params(),
        cost_estimate=pl.CostEstimate(
            flops=400_000_000, bytes_accessed=4_000_000, transcendentals=400_000
        ),
        name="space_grads",
    )(query, key, value, grad, *arrived)


def finish_kernel(steps, order_ref, *refs):
    parts, (own_ref, got0_ref, got1_ref), outs = refs[:4], refs[4:7], refs[7:]
    step = pl.program_id(0)
    share, frames = parts[0].shape[1], own_ref.shape[1]
    half = frames // 2

    @pl.when(step < steps)
    def _():
        me = lax.axis_index("space")
        for flip, part_ref in enumerate(parts):
            place = pl.ds(share * (me ^ flip), share)
            for index, out_ref in enumerate(outs):
                out_ref[place] = part_ref[index]

    @pl.when(step >= steps)
    def _():
        slots = side_slots(order_ref)
        for slot, query_ref, key_ref in zip(slots, (got0_ref, got1_ref), (got1_ref, got0_ref)):
            mine = pl.ds(slot * half, half)
            arrived = (query_ref[2], key_ref[0], key_ref[1])
            for index, (out_ref, piece) in enumerate(zip(outs, arrived)):
                out_ref[mine] = (own_ref[index, mine] + piece.astype(F32)).astype(BF16)


def finish(group_order, parts, own, got0, got1):
    _, frames, patches, columns = own.shape
    wide = 3 * LANES
    steps = columns // wide
    share = parts[0].shape[1]

    def early(i, *_):
        return (0, 0, 0, jnp.minimum(i, steps - 1))

    def late(i, *_):
        return (0, 0, 0, jnp.maximum(i - steps, 0))

    return pl.pallas_call(
        functools.partial(finish_kernel, steps),
        grid_spec=pltpu.PrefetchScalarGridSpec(
            num_scalar_prefetch=1,
            grid=(2 * steps,),
            in_specs=[pl.BlockSpec((3, share, patches, wide), early)] * 4
            + [pl.BlockSpec((3, frames, patches, wide), late)]
            + [pl.BlockSpec((3, frames // 2, patches, wide), late)] * 2,
            out_specs=[pl.BlockSpec((frames, patches, wide), lambda i, *_: (0, 0, i))] * 3,
        ),
        out_shape=[jax.ShapeDtypeStruct((frames, patches, 2 * columns), BF16)] * 3,
        compiler_params=params(),
        name="finish",
    )(group_order, *parts, own, got0, got1)


def on_device(query, key, value, grad_out, group_order, lookback):
    chain, sent = pack(group_order, query, key, value, grad_out)
    sent = list(sent)
    got = [chain_swap(part, phase) for phase, part in enumerate(chain)]
    arrived = [space_swap(part, flip) for flip, part in enumerate(sent, 1)]
    ours = chain_sums(group_order, lookback, query, key, value, grad_out, *got)
    theirs = [chain_swap(part, phase) for phase, part in enumerate(ours)]
    own, *back = chain_grads(group_order, lookback, query, key, value, grad_out, *got, ours, theirs)
    back = [chain_swap(part, phase) for phase, part in enumerate(back)]
    results = space_grads(query, key, value, grad_out, arrived)
    parts = [results[0]] + [space_swap(part, flip) for flip, part in enumerate(results[1:], 1)]
    return tuple(finish(group_order, parts, own, *back))


def solution(mesh):
    spread = P("tm", "space", None)
    return jax.shard_map(
        on_device,
        mesh=mesh,
        in_specs=(spread,) * 4 + (P(), P()),
        out_specs=(spread,) * 3,
        check_vma=False,
    )
```

```python
import functools

import jax
import jax.numpy as jnp
import numpy as np
from jax import lax
from jax.experimental import pallas as pl
from jax.experimental.pallas import tpu as pltpu
from jax.sharding import PartitionSpec as P

HD = 64
LANES = 2 * HD
CHAIN_LANES = 4 * HD
SPACE_LANES = 12 * HD
BAND = 16
FACTOR = HD**-0.5
VMEM_LIMIT = 48 * 1024 * 1024
BF16 = jnp.bfloat16
F32 = jnp.float32


def params(**kwargs):
    return pltpu.CompilerParams(vmem_limit_bytes=VMEM_LIMIT, **kwargs)


def chain_swap(value, phase):
    count = lax.axis_size("tm")
    pairs = []
    for source in range(count):
        target = source ^ 1 if phase == 0 else ((source + 1) ^ 1) - 1
        if target == count:
            target = source
        if target >= 0:
            pairs.append((source, target))
    return lax.ppermute(value, "tm", pairs)


def space_swap(value, flip):
    count = lax.axis_size("space")
    return lax.ppermute(value, "space", [(i, i ^ flip) for i in range(count)])


def side_slots(order_ref):
    device = lax.axis_index("tm")
    early_slot = jnp.where(order_ref[2 * device] == device, 0, 1)
    odd = lax.rem(device, 2)
    slot0 = jnp.where(odd == 1, early_slot, 1 - early_slot)
    return slot0, 1 - slot0


def side_groups(entries):
    device = lax.axis_index("tm")
    odd = lax.rem(device, 2)
    late = entries - 1 - device
    return jnp.where(odd == 1, device, late), jnp.where(odd == 1, late, device)


def pack_kernel(order_ref, query_ref, key_ref, value_ref, grad_ref, *refs):
    chain_refs, space_refs, sems = refs[:2], refs[2:5], refs[5]
    slot0, slot1 = side_slots(order_ref)
    me = lax.axis_index("space")
    frames, _, width = key_ref.shape
    half, share, columns = frames // 2, frames // 4, width // 2
    copies = []

    def send(source, first, count, column, target):
        piece = source.at[pl.ds(first, count), :, pl.ds(column, columns)]
        copies.append(pltpu.make_async_copy(piece, target, sems.at[len(copies)]))

    for here, there, out_ref in ((slot0, slot1, chain_refs[0]), (slot1, slot0, chain_refs[1])):
        send(key_ref, there * half, half, columns, out_ref.at[0])
        send(value_ref, there * half, half, columns, out_ref.at[1])
        send(query_ref, here * half, half, columns, out_ref.at[2])
        send(grad_ref, here * half, half, columns, out_ref.at[3])
    for flip, out_ref in enumerate(space_refs, 1):
        for part, source in enumerate((query_ref, key_ref, value_ref, grad_ref)):
            send(source, (me ^ flip) * share, share, 0, out_ref.at[part])
    for copy in copies:
        copy.start()
    for copy in copies:
        copy.wait()


def pack(group_order, query, key, value, grad):
    frames, patches, width = key.shape
    chain = jax.ShapeDtypeStruct((4, frames // 2, patches, width // 2), BF16)
    space = jax.ShapeDtypeStruct((4, frames // 4, patches, width // 2), BF16)
    outs = pl.pallas_call(
        pack_kernel,
        out_shape=(chain, chain, space, space, space),
        in_specs=[pl.BlockSpec(memory_space=pltpu.SMEM)] + [pl.BlockSpec(memory_space=pl.ANY)] * 4,
        out_specs=[pl.BlockSpec(memory_space=pl.ANY)] * 5,
        scratch_shapes=[pltpu.SemaphoreType.DMA((20,))],
        compiler_params=params(),
        name="pack",
    )(*[pltpu.with_memory_space_constraint(x, pltpu.HBM) for x in (group_order, query, key, value, grad)])
    return outs[:2], outs[2:]


def per_head(rows):
    head = lax.broadcasted_iota(jnp.int32, rows.shape, 1) // HD
    zero = jnp.zeros_like(rows)
    return jnp.concatenate([jnp.where(head == h, rows, zero) for h in range(rows.shape[1] // HD)], axis=0)


def own_head(bands):
    heads = bands.shape[1] // HD
    rows = bands.shape[0] // heads
    head = lax.broadcasted_iota(jnp.int32, (rows, bands.shape[1]), 1) // HD
    result = bands[:rows]
    for h in range(1, heads):
        result = jnp.where(head == h, bands[h * rows : (h + 1) * rows], result)
    return result


BY_ROWS = (((1,), (1,)), ((), ()))
BY_COLUMNS = (((0,), (0,)), ((), ()))


def pairs(key, value, scaled, grads, weight):
    unnormed = jnp.exp(lax.dot_general(key, scaled, BY_ROWS, preferred_element_type=F32))
    if weight is not None:
        unnormed = unnormed * weight
    return unnormed, lax.dot_general(value, grads, BY_ROWS, preferred_element_type=F32)


def sums(unnormed, grad_probs):
    return jnp.sum(unnormed, axis=0, keepdims=True), jnp.sum(unnormed * grad_probs, axis=0, keepdims=True)


def gradients(key, scaled, grads, unnormed, grad_probs, totals, weighted):
    inverse = jnp.where(totals > 0.0, 1.0 / totals, 0.0)
    prob = unnormed * inverse
    grad_scores = (prob * (grad_probs - weighted * inverse)).astype(BF16)
    grad_value = jnp.dot(prob.astype(BF16), grads, preferred_element_type=F32)
    grad_key = jnp.dot(grad_scores, scaled, preferred_element_type=F32)
    bands = lax.dot_general(grad_scores, key, BY_COLUMNS, preferred_element_type=F32)
    return own_head(bands) * FACTOR, grad_key, grad_value


def scale(query):
    return per_head(query * jnp.asarray(FACTOR, BF16))


def attend(query, key, value, grad):
    scaled, grads = scale(query), per_head(grad)
    unnormed, grad_probs = pairs(key, value, scaled, grads, None)
    return gradients(key, scaled, grads, unnormed, grad_probs, *sums(unnormed, grad_probs))


class Side:
    def __init__(self, side, order_ref, lookback_ref, locals_, before_ref, after_ref):
        self.locals, self.before, self.after = locals_, before_ref, after_ref
        frames, self.patches, width = locals_[0].shape
        self.lanes = CHAIN_LANES
        self.first = width // 2
        self.half = frames // 2
        self.rows = self.half * BAND
        self.heads = self.lanes // HD
        self.mine = pl.ds(side_slots(order_ref)[side] * self.half, self.half)
        entries = order_ref.shape[0]
        group = side_groups(entries)[side]
        reach = jnp.minimum(lookback_ref[group], group)
        following = jnp.minimum(group + 1, entries - 1)
        reach_after = jnp.where(group + 1 < entries, jnp.minimum(lookback_ref[following], following), 0)
        shape = (2 * self.rows, self.heads * self.rows)
        key_row = lax.broadcasted_iota(jnp.int32, shape, 0)
        query_row = lax.broadcasted_iota(jnp.int32, shape, 1)
        same = lax.rem(key_row, BAND) == lax.rem(query_row, BAND)
        allowed = same & (key_row // self.rows <= reach)
        self.weight = jnp.where(allowed, 1.0, 0.0)
        self.skip_weight = jnp.where(same & (reach_after >= 2), 1.0, 0.0)[: self.rows]

    def flat(self, piece):
        return piece.reshape(self.rows, self.lanes)

    def load(self, quad, band):
        at = pl.ds(band * BAND, BAND)
        near, far = pl.ds(self.first + quad * self.lanes, self.lanes), pl.ds(quad * self.lanes, self.lanes)
        query, key, value, grad = (self.flat(ref[self.mine, at, near]) for ref in self.locals)
        key_before, value_before = (self.flat(self.before[index, :, at, far]) for index in (0, 1))
        query_after, grad_after = (self.flat(self.after[index, :, at, far]) for index in (2, 3))
        keys = jnp.concatenate([key, key_before], axis=0)
        values = jnp.concatenate([value, value_before], axis=0)
        near = (keys, scale(query), per_head(grad))
        skip = (key_before, scale(query_after), per_head(grad_after))
        near_pairs = pairs(keys, values, near[1], near[2], self.weight)
        skip_pairs = pairs(key_before, value_before, skip[1], skip[2], self.skip_weight)
        return near + near_pairs, skip + skip_pairs


def both_sides(order_ref, lookback_ref, locals_, got0_ref, got1_ref):
    return (
        Side(0, order_ref, lookback_ref, locals_, got0_ref, got1_ref),
        Side(1, order_ref, lookback_ref, locals_, got1_ref, got0_ref),
    )


def chain_sums_kernel(
    order_ref, lookback_ref, query_ref, key_ref, value_ref, grad_ref, got0_ref, got1_ref, out0_ref, out1_ref
):
    sides = both_sides(order_ref, lookback_ref, (query_ref, key_ref, value_ref, grad_ref), got0_ref, got1_ref)
    for side, near_out, skip_out in zip(sides, (out0_ref, out1_ref), (out1_ref, out0_ref)):
        for quad, band in np.ndindex(*out0_ref.shape[:2]):
            near, skip = side.load(quad, band)
            near_out[quad, band, 0:1], near_out[quad, band, 1:2] = sums(*near[3:])
            skip_out[quad, band, 2:3], skip_out[quad, band, 3:4] = sums(*skip[3:])


def chain_grads_kernel(
    order_ref,
    lookback_ref,
    query_ref,
    key_ref,
    value_ref,
    grad_ref,
    got0_ref,
    got1_ref,
    sums0_ref,
    sums1_ref,
    from0_ref,
    from1_ref,
    own_ref,
    out0_ref,
    out1_ref,
):
    sides = both_sides(order_ref, lookback_ref, (query_ref, key_ref, value_ref, grad_ref), got0_ref, got1_ref)
    mine, others, outs = (sums0_ref, sums1_ref), (from0_ref, from1_ref), (out0_ref, out1_ref)
    for number, side in enumerate(sides):
        rows, tall = side.rows, (side.half, BAND, side.lanes)
        for quad, band in np.ndindex(*sums0_ref.shape[:2]):
            at, far = pl.ds(band * BAND, BAND), pl.ds(quad * CHAIN_LANES, CHAIN_LANES)
            near, skip = side.load(quad, band)

            def whole_sums(row):
                place = number if row == 0 else 1 - number
                ours, theirs = mine[place], others[place]
                return [
                    ours[quad, band, row + k : row + k + 1] + theirs[quad, band, 2 - row + k : 3 - row + k] for k in (0, 1)
                ]

            dq, dk, dv = gradients(*near, *whole_sums(0))
            dq_after, dk_before, dv_before = gradients(*skip, *whole_sums(2))
            own_ref[0, side.mine, at, far] = dq.reshape(tall)
            own_ref[1, side.mine, at, far] = dk[:rows].reshape(tall)
            own_ref[2, side.mine, at, far] = dv[:rows].reshape(tall)
            back, on = outs[number], outs[1 - number]
            back[0, :, at, far] = (dk[rows:] + dk_before).astype(BF16).reshape(tall)
            back[1, :, at, far] = (dv[rows:] + dv_before).astype(BF16).reshape(tall)
            on[2, :, at, far] = dq_after.astype(BF16).reshape(tall)


def chain_call(kernel, out_shape, name, *operands):
    return pl.pallas_call(
        kernel,
        in_specs=[pl.BlockSpec(memory_space=pltpu.SMEM)] * 2
        + [pl.BlockSpec(memory_space=pltpu.VMEM)] * (len(operands) - 2),
        out_specs=[pl.BlockSpec(memory_space=pltpu.VMEM)] * len(out_shape),
        out_shape=out_shape,
        compiler_params=params(),
        name=name,
    )(*operands)


def chain_sums(group_order, lookback, query, key, value, grad, got0, got1):
    frames, patches, width = query.shape
    steps, bands = width // 2 // CHAIN_LANES, patches // BAND
    shape = jax.ShapeDtypeStruct((steps, bands, 4, CHAIN_LANES // HD * frames // 2 * BAND), F32)
    operands = (group_order, lookback, query, key, value, grad, got0, got1)
    return chain_call(chain_sums_kernel, [shape] * 2, "chain_sums", *operands)


def chain_grads(group_order, lookback, query, key, value, grad, got0, got1, ours, theirs):
    frames, patches, width = query.shape
    half, columns = frames // 2, width // 2
    sent = jax.ShapeDtypeStruct((3, half, patches, columns), BF16)
    shapes = [jax.ShapeDtypeStruct((3, frames, patches, columns), F32), sent, sent]
    operands = (group_order, lookback, query, key, value, grad, got0, got1, *ours, *theirs)
    return chain_call(chain_grads_kernel, shapes, "chain_grads", *operands)


def space_kernel(
    query_ref, key_ref, value_ref, grad_ref, in1_ref, in2_ref, in3_ref, out0_ref, out1_ref, out2_ref, out3_ref
):
    me = lax.axis_index("space")
    share, patches = in1_ref.shape[1], in1_ref.shape[2]
    outs = (out0_ref, out1_ref, out2_ref, out3_ref)
    for frame in range(share):
        gathered = [
            jnp.concatenate(
                [own_ref[share * me + frame]] + [ref[part, frame] for ref in (in1_ref, in2_ref, in3_ref)],
                axis=0,
            )
            for part, own_ref in enumerate((query_ref, key_ref, value_ref, grad_ref))
        ]
        couples = [
            attend(*(rows[:, c : c + LANES] for rows in gathered))
            for c in range(0, gathered[0].shape[1], LANES)
        ]
        grad_query, grad_key, grad_value = (jnp.concatenate(x, axis=1) for x in zip(*couples))
        for part, result in enumerate((grad_query, grad_key, grad_value)):
            result = result.astype(BF16)
            for place, out_ref in enumerate(outs):
                out_ref[part, frame] = result[place * patches : (place + 1) * patches]


def space_grads(query, key, value, grad, arrived):
    frames, patches, width = query.shape
    share, columns = frames // 4, width // 2
    own = pl.BlockSpec((frames, patches, SPACE_LANES), lambda i: (0, 0, i))
    return pl.pallas_call(
        space_kernel,
        grid=(columns // SPACE_LANES,),
        in_specs=[own] * 4 + [pl.BlockSpec((4, share, patches, SPACE_LANES), lambda i: (0, 0, 0, i))] * 3,
        out_specs=[pl.BlockSpec((3, share, patches, SPACE_LANES), lambda i: (0, 0, 0, i))] * 4,
        out_shape=[jax.ShapeDtypeStruct((3, share, patches, columns), BF16)] * 4,
        compiler_params=params(),
        cost_estimate=pl.CostEstimate(
            flops=400_000_000, bytes_accessed=4_000_000, transcendentals=400_000
        ),
        name="space_grads",
    )(query, key, value, grad, *arrived)


def finish_chain_kernel(order_ref, own_ref, got0_ref, got1_ref, *outs):
    half = own_ref.shape[1] // 2
    slots = side_slots(order_ref)
    for slot, query_ref, key_ref in zip(slots, (got0_ref, got1_ref), (got1_ref, got0_ref)):
        mine = pl.ds(slot * half, half)
        arrived = (query_ref[2], key_ref[0], key_ref[1])
        for index, (out_ref, piece) in enumerate(zip(outs, arrived)):
            out_ref[mine] = (own_ref[index, mine] + piece.astype(F32)).astype(BF16)


def finish_chain(group_order, own, got0, got1):
    _, frames, patches, columns = own.shape
    wide = 3 * LANES
    steps = columns // wide
    return pl.pallas_call(
        finish_chain_kernel,
        grid_spec=pltpu.PrefetchScalarGridSpec(
            num_scalar_prefetch=1,
            grid=(steps,),
            in_specs=[pl.BlockSpec((3, frames, patches, wide), lambda i, *_: (0, 0, 0, i))]
            + [pl.BlockSpec((3, frames // 2, patches, wide), lambda i, *_: (0, 0, 0, i))] * 2,
            out_specs=[pl.BlockSpec((frames, patches, wide), lambda i, *_: (0, 0, steps + i))] * 3,
        ),
        out_shape=[jax.ShapeDtypeStruct((frames, patches, 2 * columns), BF16)] * 3,
        compiler_params=params(),
        name="finish_chain",
    )(group_order, own, got0, got1)


def finish_space_kernel(*refs):
    parts, outs = refs[:4], refs[7:]
    me = lax.axis_index("space")
    share = parts[0].shape[1]
    for flip, part_ref in enumerate(parts):
        place = pl.ds(share * (me ^ flip), share)
        for index, out_ref in enumerate(outs):
            out_ref[place] = part_ref[index]


def finish_space(parts, outs):
    _, share, patches, columns = parts[0].shape
    frames, wide = 4 * share, 3 * LANES
    return pl.pallas_call(
        finish_space_kernel,
        grid=(columns // wide,),
        in_specs=[pl.BlockSpec((3, share, patches, wide), lambda i: (0, 0, 0, i))] * 4
        + [pl.BlockSpec(memory_space=pl.ANY)] * 3,
        out_specs=[pl.BlockSpec((frames, patches, wide), lambda i: (0, 0, i))] * 3,
        out_shape=[jax.ShapeDtypeStruct(array.shape, BF16) for array in outs],
        input_output_aliases={4: 0, 5: 1, 6: 2},
        compiler_params=params(),
        name="finish_space",
    )(*parts, *outs)


def on_device(query, key, value, grad_out, group_order, lookback):
    chain, sent = pack(group_order, query, key, value, grad_out)
    arrived = [space_swap(part, flip) for flip, part in enumerate(sent, 1)]
    got = [chain_swap(part, phase) for phase, part in enumerate(chain)]
    ours = chain_sums(group_order, lookback, query, key, value, grad_out, *got)
    theirs = [chain_swap(part, phase) for phase, part in enumerate(ours)]
    own, *back = chain_grads(group_order, lookback, query, key, value, grad_out, *got, ours, theirs)
    results = space_grads(query, key, value, grad_out, arrived)
    parts = [results[0]] + [space_swap(part, flip) for flip, part in enumerate(results[1:], 1)]
    back = [chain_swap(part, phase) for phase, part in enumerate(back)]
    return tuple(finish_space(parts, finish_chain(group_order, own, *back)))


def solution(mesh):
    spread = P("tm", "space", None)
    return jax.shard_map(
        on_device,
        mesh=mesh,
        in_specs=(spread,) * 4 + (P(), P()),
        out_specs=(spread,) * 3,
        check_vma=False,
    )
```

```python
import functools

import jax
import jax.numpy as jnp
import numpy as np
from jax import lax
from jax.experimental import pallas as pl
from jax.experimental.pallas import tpu as pltpu
from jax.sharding import PartitionSpec as P

HD = 64
LANES = 2 * HD
CHAIN_LANES = 4 * HD
SPACE_LANES = 12 * HD
BAND = 16
FACTOR = HD**-0.5
VMEM_LIMIT = 48 * 1024 * 1024
BF16 = jnp.bfloat16
F32 = jnp.float32


def params(**kwargs):
    return pltpu.CompilerParams(vmem_limit_bytes=VMEM_LIMIT, **kwargs)


def chain_swap(value, phase):
    count = lax.axis_size("tm")
    pairs = []
    for source in range(count):
        target = source ^ 1 if phase == 0 else ((source + 1) ^ 1) - 1
        if target == count:
            target = source
        if target >= 0:
            pairs.append((source, target))
    return lax.ppermute(value, "tm", pairs)


def space_swap(value, flip):
    count = lax.axis_size("space")
    return lax.ppermute(value, "space", [(i, i ^ flip) for i in range(count)])


def side_slots(order_ref):
    device = lax.axis_index("tm")
    early_slot = jnp.where(order_ref[2 * device] == device, 0, 1)
    odd = lax.rem(device, 2)
    slot0 = jnp.where(odd == 1, early_slot, 1 - early_slot)
    return slot0, 1 - slot0


def side_groups(entries):
    device = lax.axis_index("tm")
    odd = lax.rem(device, 2)
    late = entries - 1 - device
    return jnp.where(odd == 1, device, late), jnp.where(odd == 1, late, device)


def pack_chain_kernel(order_ref, query_ref, key_ref, value_ref, grad_ref, out0_ref, out1_ref, sems):
    slot0, slot1 = side_slots(order_ref)
    frames, _, width = key_ref.shape
    half, columns = frames // 2, pl.ds(width // 2, width // 2)
    copies = []
    for here, there, out_ref in ((slot0, slot1, out0_ref), (slot1, slot0, out1_ref)):
        pieces = ((key_ref, there), (value_ref, there), (query_ref, here), (grad_ref, here))
        for part, (source, slot) in enumerate(pieces):
            piece = source.at[pl.ds(slot * half, half), :, columns]
            copies.append(pltpu.make_async_copy(piece, out_ref.at[part], sems.at[len(copies)]))
    for copy in copies:
        copy.start()
    for copy in copies:
        copy.wait()


def pack_space_kernel(*refs):
    arrays, outs, sems = refs[:4], refs[4:7], refs[7]
    me = lax.axis_index("space")
    share, columns = outs[0].shape[1], pl.ds(0, outs[0].shape[3])
    copies = []
    for flip, out_ref in enumerate(outs, 1):
        for part, source in enumerate(arrays):
            piece = source.at[pl.ds((me ^ flip) * share, share), :, columns]
            copies.append(pltpu.make_async_copy(piece, out_ref.at[part], sems.at[len(copies)]))
    for copy in copies:
        copy.start()
    for copy in copies:
        copy.wait()


def pack(kernel, shapes, copies, scalars, arrays, name):
    return pl.pallas_call(
        kernel,
        out_shape=shapes,
        in_specs=[pl.BlockSpec(memory_space=pltpu.SMEM)] * len(scalars)
        + [pl.BlockSpec(memory_space=pl.ANY)] * len(arrays),
        out_specs=[pl.BlockSpec(memory_space=pl.ANY)] * len(shapes),
        scratch_shapes=[pltpu.SemaphoreType.DMA((copies,))],
        compiler_params=params(),
        name=name,
    )(*[pltpu.with_memory_space_constraint(x, pltpu.HBM) for x in (*scalars, *arrays)])


def pack_all(group_order, *arrays):
    frames, patches, width = arrays[0].shape
    chain = jax.ShapeDtypeStruct((4, frames // 2, patches, width // 2), BF16)
    space = jax.ShapeDtypeStruct((4, frames // 4, patches, width // 2), BF16)
    return (
        pack(pack_chain_kernel, [chain] * 2, 8, (group_order,), arrays, "pack_chain"),
        pack(pack_space_kernel, [space] * 3, 12, (), arrays, "pack_space"),
    )


def per_head(rows):
    head = lax.broadcasted_iota(jnp.int32, rows.shape, 1) // HD
    zero = jnp.zeros_like(rows)
    return jnp.concatenate([jnp.where(head == h, rows, zero) for h in range(rows.shape[1] // HD)], axis=0)


def own_head(bands):
    heads = bands.shape[1] // HD
    rows = bands.shape[0] // heads
    head = lax.broadcasted_iota(jnp.int32, (rows, bands.shape[1]), 1) // HD
    result = bands[:rows]
    for h in range(1, heads):
        result = jnp.where(head == h, bands[h * rows : (h + 1) * rows], result)
    return result


BY_ROWS = (((1,), (1,)), ((), ()))
BY_COLUMNS = (((0,), (0,)), ((), ()))


def pairs(key, value, scaled, grads, weight):
    unnormed = jnp.exp(lax.dot_general(key, scaled, BY_ROWS, preferred_element_type=F32))
    if weight is not None:
        unnormed = unnormed * weight
    return unnormed, lax.dot_general(value, grads, BY_ROWS, preferred_element_type=F32)


def sums(unnormed, grad_probs):
    return jnp.sum(unnormed, axis=0, keepdims=True), jnp.sum(unnormed * grad_probs, axis=0, keepdims=True)


def gradients(key, scaled, grads, unnormed, grad_probs, totals, weighted):
    inverse = jnp.where(totals > 0.0, 1.0 / totals, 0.0)
    prob = unnormed * inverse
    grad_scores = (prob * (grad_probs - weighted * inverse)).astype(BF16)
    grad_value = jnp.dot(prob.astype(BF16), grads, preferred_element_type=F32)
    grad_key = jnp.dot(grad_scores, scaled, preferred_element_type=F32)
    bands = lax.dot_general(grad_scores, key, BY_COLUMNS, preferred_element_type=F32)
    return own_head(bands) * FACTOR, grad_key, grad_value


def scale(query):
    return per_head(query * jnp.asarray(FACTOR, BF16))


def attend(query, key, value, grad):
    scaled, grads = scale(query), per_head(grad)
    unnormed, grad_probs = pairs(key, value, scaled, grads, None)
    return gradients(key, scaled, grads, unnormed, grad_probs, *sums(unnormed, grad_probs))


class Side:
    def __init__(self, side, order_ref, lookback_ref, locals_, before_ref, after_ref):
        self.locals, self.before, self.after = locals_, before_ref, after_ref
        frames, self.patches, width = locals_[0].shape
        self.lanes = CHAIN_LANES
        self.first = width // 2
        self.half = frames // 2
        self.rows = self.half * BAND
        self.heads = self.lanes // HD
        self.mine = pl.ds(side_slots(order_ref)[side] * self.half, self.half)
        entries = order_ref.shape[0]
        group = side_groups(entries)[side]
        reach = jnp.minimum(lookback_ref[group], group)
        following = jnp.minimum(group + 1, entries - 1)
        reach_after = jnp.where(group + 1 < entries, jnp.minimum(lookback_ref[following], following), 0)
        shape = (2 * self.rows, self.heads * self.rows)
        key_row = lax.broadcasted_iota(jnp.int32, shape, 0)
        query_row = lax.broadcasted_iota(jnp.int32, shape, 1)
        same = lax.rem(key_row, BAND) == lax.rem(query_row, BAND)
        allowed = same & (key_row // self.rows <= reach)
        self.weight = jnp.where(allowed, 1.0, 0.0)
        self.skip_weight = jnp.where(same & (reach_after >= 2), 1.0, 0.0)[: self.rows]

    def flat(self, piece):
        return piece.reshape(self.rows, self.lanes)

    def load(self, quad, band):
        at = pl.ds(band * BAND, BAND)
        near, far = pl.ds(self.first + quad * self.lanes, self.lanes), pl.ds(quad * self.lanes, self.lanes)
        query, key, value, grad = (self.flat(ref[self.mine, at, near]) for ref in self.locals)
        key_before, value_before = (self.flat(self.before[index, :, at, far]) for index in (0, 1))
        query_after, grad_after = (self.flat(self.after[index, :, at, far]) for index in (2, 3))
        keys = jnp.concatenate([key, key_before], axis=0)
        values = jnp.concatenate([value, value_before], axis=0)
        near = (keys, scale(query), per_head(grad))
        skip = (key_before, scale(query_after), per_head(grad_after))
        near_pairs = pairs(keys, values, near[1], near[2], self.weight)
        skip_pairs = pairs(key_before, value_before, skip[1], skip[2], self.skip_weight)
        return near + near_pairs, skip + skip_pairs


def both_sides(order_ref, lookback_ref, locals_, got0_ref, got1_ref):
    return (
        Side(0, order_ref, lookback_ref, locals_, got0_ref, got1_ref),
        Side(1, order_ref, lookback_ref, locals_, got1_ref, got0_ref),
    )


def chain_sums_kernel(
    order_ref, lookback_ref, query_ref, key_ref, value_ref, grad_ref, got0_ref, got1_ref, out0_ref, out1_ref
):
    sides = both_sides(order_ref, lookback_ref, (query_ref, key_ref, value_ref, grad_ref), got0_ref, got1_ref)
    for side, near_out, skip_out in zip(sides, (out0_ref, out1_ref), (out1_ref, out0_ref)):
        for quad, band in np.ndindex(*out0_ref.shape[:2]):
            near, skip = side.load(quad, band)
            near_out[quad, band, 0:1], near_out[quad, band, 1:2] = sums(*near[3:])
            skip_out[quad, band, 2:3], skip_out[quad, band, 3:4] = sums(*skip[3:])


def chain_grads_kernel(
    order_ref,
    lookback_ref,
    query_ref,
    key_ref,
    value_ref,
    grad_ref,
    got0_ref,
    got1_ref,
    sums0_ref,
    sums1_ref,
    from0_ref,
    from1_ref,
    own_ref,
    out0_ref,
    out1_ref,
):
    sides = both_sides(order_ref, lookback_ref, (query_ref, key_ref, value_ref, grad_ref), got0_ref, got1_ref)
    mine, others, outs = (sums0_ref, sums1_ref), (from0_ref, from1_ref), (out0_ref, out1_ref)
    for number, side in enumerate(sides):
        rows, tall = side.rows, (side.half, BAND, side.lanes)
        for quad, band in np.ndindex(*sums0_ref.shape[:2]):
            at, far = pl.ds(band * BAND, BAND), pl.ds(quad * CHAIN_LANES, CHAIN_LANES)
            near, skip = side.load(quad, band)

            def whole_sums(row):
                place = number if row == 0 else 1 - number
                ours, theirs = mine[place], others[place]
                return [
                    ours[quad, band, row + k : row + k + 1] + theirs[quad, band, 2 - row + k : 3 - row + k] for k in (0, 1)
                ]

            dq, dk, dv = gradients(*near, *whole_sums(0))
            dq_after, dk_before, dv_before = gradients(*skip, *whole_sums(2))
            own_ref[0, side.mine, at, far] = dq.reshape(tall)
            own_ref[1, side.mine, at, far] = dk[:rows].reshape(tall)
            own_ref[2, side.mine, at, far] = dv[:rows].reshape(tall)
            back, on = outs[number], outs[1 - number]
            back[0, :, at, far] = (dk[rows:] + dk_before).astype(BF16).reshape(tall)
            back[1, :, at, far] = (dv[rows:] + dv_before).astype(BF16).reshape(tall)
            on[2, :, at, far] = dq_after.astype(BF16).reshape(tall)


def chain_call(kernel, out_shape, name, *operands):
    return pl.pallas_call(
        kernel,
        in_specs=[pl.BlockSpec(memory_space=pltpu.SMEM)] * 2
        + [pl.BlockSpec(memory_space=pltpu.VMEM)] * (len(operands) - 2),
        out_specs=[pl.BlockSpec(memory_space=pltpu.VMEM)] * len(out_shape),
        out_shape=out_shape,
        compiler_params=params(),
        name=name,
    )(*operands)


def chain_sums(group_order, lookback, query, key, value, grad, got0, got1):
    frames, patches, width = query.shape
    steps, bands = width // 2 // CHAIN_LANES, patches // BAND
    shape = jax.ShapeDtypeStruct((steps, bands, 4, CHAIN_LANES // HD * frames // 2 * BAND), F32)
    operands = (group_order, lookback, query, key, value, grad, got0, got1)
    return chain_call(chain_sums_kernel, [shape] * 2, "chain_sums", *operands)


def chain_grads(group_order, lookback, query, key, value, grad, got0, got1, ours, theirs):
    frames, patches, width = query.shape
    half, columns = frames // 2, width // 2
    sent = jax.ShapeDtypeStruct((3, half, patches, columns), BF16)
    shapes = [jax.ShapeDtypeStruct((3, frames, patches, columns), F32), sent, sent]
    operands = (group_order, lookback, query, key, value, grad, got0, got1, *ours, *theirs)
    return chain_call(chain_grads_kernel, shapes, "chain_grads", *operands)


def space_kernel(
    query_ref, key_ref, value_ref, grad_ref, in1_ref, in2_ref, in3_ref, out0_ref, out1_ref, out2_ref, out3_ref
):
    me = lax.axis_index("space")
    share, patches = in1_ref.shape[1], in1_ref.shape[2]
    outs = (out0_ref, out1_ref, out2_ref, out3_ref)
    for frame in range(share):
        gathered = [
            jnp.concatenate(
                [own_ref[share * me + frame]] + [ref[part, frame] for ref in (in1_ref, in2_ref, in3_ref)],
                axis=0,
            )
            for part, own_ref in enumerate((query_ref, key_ref, value_ref, grad_ref))
        ]
        couples = [
            attend(*(rows[:, c : c + LANES] for rows in gathered))
            for c in range(0, gathered[0].shape[1], LANES)
        ]
        grad_query, grad_key, grad_value = (jnp.concatenate(x, axis=1) for x in zip(*couples))
        for part, result in enumerate((grad_query, grad_key, grad_value)):
            result = result.astype(BF16)
            for place, out_ref in enumerate(outs):
                out_ref[part, frame] = result[place * patches : (place + 1) * patches]


def space_grads(query, key, value, grad, arrived):
    frames, patches, width = query.shape
    share, columns = frames // 4, width // 2
    own = pl.BlockSpec((frames, patches, SPACE_LANES), lambda i: (0, 0, i))
    return pl.pallas_call(
        space_kernel,
        grid=(columns // SPACE_LANES,),
        in_specs=[own] * 4 + [pl.BlockSpec((4, share, patches, SPACE_LANES), lambda i: (0, 0, 0, i))] * 3,
        out_specs=[pl.BlockSpec((3, share, patches, SPACE_LANES), lambda i: (0, 0, 0, i))] * 4,
        out_shape=[jax.ShapeDtypeStruct((3, share, patches, columns), BF16)] * 4,
        compiler_params=params(),
        cost_estimate=pl.CostEstimate(
            flops=400_000_000, bytes_accessed=4_000_000, transcendentals=400_000
        ),
        name="space_grads",
    )(query, key, value, grad, *arrived)


def finish_chain_kernel(order_ref, own_ref, got0_ref, got1_ref, *outs):
    half = own_ref.shape[1] // 2
    slots = side_slots(order_ref)
    for slot, query_ref, key_ref in zip(slots, (got0_ref, got1_ref), (got1_ref, got0_ref)):
        mine = pl.ds(slot * half, half)
        arrived = (query_ref[2], key_ref[0], key_ref[1])
        for index, (out_ref, piece) in enumerate(zip(outs, arrived)):
            out_ref[mine] = (own_ref[index, mine] + piece.astype(F32)).astype(BF16)


def finish_chain(group_order, own, got0, got1):
    _, frames, patches, columns = own.shape
    wide = 3 * LANES
    steps = columns // wide
    return pl.pallas_call(
        finish_chain_kernel,
        grid_spec=pltpu.PrefetchScalarGridSpec(
            num_scalar_prefetch=1,
            grid=(steps,),
            in_specs=[pl.BlockSpec((3, frames, patches, wide), lambda i, *_: (0, 0, 0, i))]
            + [pl.BlockSpec((3, frames // 2, patches, wide), lambda i, *_: (0, 0, 0, i))] * 2,
            out_specs=[pl.BlockSpec((frames, patches, wide), lambda i, *_: (0, 0, steps + i))] * 3,
        ),
        out_shape=[jax.ShapeDtypeStruct((frames, patches, 2 * columns), BF16)] * 3,
        compiler_params=params(),
        name="finish_chain",
    )(group_order, own, got0, got1)


def finish_space_kernel(*refs):
    parts, outs = refs[:4], refs[7:]
    me = lax.axis_index("space")
    share = parts[0].shape[1]
    for flip, part_ref in enumerate(parts):
        place = pl.ds(share * (me ^ flip), share)
        for index, out_ref in enumerate(outs):
            out_ref[place] = part_ref[index]


def finish_space(parts, outs):
    _, share, patches, columns = parts[0].shape
    frames, wide = 4 * share, 3 * LANES
    return pl.pallas_call(
        finish_space_kernel,
        grid=(columns // wide,),
        in_specs=[pl.BlockSpec((3, share, patches, wide), lambda i: (0, 0, 0, i))] * 4
        + [pl.BlockSpec(memory_space=pl.ANY)] * 3,
        out_specs=[pl.BlockSpec((frames, patches, wide), lambda i: (0, 0, i))] * 3,
        out_shape=[jax.ShapeDtypeStruct(array.shape, BF16) for array in outs],
        input_output_aliases={4: 0, 5: 1, 6: 2},
        compiler_params=params(),
        name="finish_space",
    )(*parts, *outs)


def on_device(query, key, value, grad_out, group_order, lookback):
    chain, sent = pack_all(group_order, query, key, value, grad_out)
    arrived = [space_swap(part, flip) for flip, part in enumerate(sent, 1)]
    got = [chain_swap(part, phase) for phase, part in enumerate(chain)]
    ours = chain_sums(group_order, lookback, query, key, value, grad_out, *got)
    theirs = [chain_swap(part, phase) for phase, part in enumerate(ours)]
    own, *back = chain_grads(group_order, lookback, query, key, value, grad_out, *got, ours, theirs)
    results = space_grads(query, key, value, grad_out, arrived)
    parts = [results[0]] + [space_swap(part, flip) for flip, part in enumerate(results[1:], 1)]
    back = [chain_swap(part, phase) for phase, part in enumerate(back)]
    return tuple(finish_space(parts, finish_chain(group_order, own, *back)))


def solution(mesh):
    spread = P("tm", "space", None)
    return jax.shard_map(
        on_device,
        mesh=mesh,
        in_specs=(spread,) * 4 + (P(), P()),
        out_specs=(spread,) * 3,
        check_vma=False,
    )
```
